32 devices in a mesh: dp: 2 (over y), expert: 16 (over z, x, core).
Axes of the slice: x: 2, y: 2, z: 4, core: 2. Of those that a mesh axis runs over, the one named last changes fastest.
Arguments:
- tokens: bfloat16 [1024, 2048], P(('dp', 'expert')), may hold values from -6 to 6
- route_weight: float32 [1024, 8], P(('dp', 'expert')), may hold values from 0.03 to 0.4
- upstream: bfloat16 [1024, 2048], P(('dp', 'expert')), may hold values from -6 to 6
- expert_index: int32 [1024, 8], P(('dp', 'expert')), may hold values from 0 to 15, all different within a row; in each aligned block of 32 rows (0 to 31, 32 to 63, ...) at most 20 rows name the same one
- gate_weight: bfloat16 [16, 2048, 768], P('expert', 'dp'), may hold values from -0.125 to 0.125
- up_weight: bfloat16 [16, 2048, 768], P('expert', 'dp'), may hold values from -0.125 to 0.125
- down_weight: bfloat16 [16, 2048, 768], P('expert', 'dp'), may hold values from -0.21875 to 0.21875
Outputs:
- combined: bfloat16 [1024, 2048], P(('dp', 'expert'))
- token_grad: bfloat16 [1024, 2048], P(('dp', 'expert'))
- route_grad: float32 [1024, 8], P(('dp', 'expert'))
- down_grad: bfloat16 [16, 2048, 768], P('expert', 'dp')
The draws below stay inside these ranges and needn't reach their ends.
Inputs may be any that keep to these rules, and one draw needn't show every extreme that they name: `expert_index`: each row names 8 different experts. Among the rows of one device no expert is named more than 20 times, and in every draw some device names some expert exactly 20 times.
All inputs are finite; a program needn't handle non-finite values.
Results may differ from the reference program's by a relative error of at most 0.017.
Values may be sent and summed in bfloat16 or wider, within the bound.
No kernel may reach another device: no remote copies, remote signals or barrier semaphores. Data moves between devices by JAX's collectives and lax.ppermute only.
A program may use at most 128 MiB of HBM per device.

```python
import math
import jax
import jax.numpy as jnp
import numpy as np
from jax import lax

D = 2048
FF = 768
TOPK = 8
TOK_DEV = 32
EXPERTS = 16
TOKENS = 1024
CAP = 20
N_DP = 2
N_EXPERT = 16


def block_scale(stream_key, shape, cuts, least, top_value):
    gain, own = 1.0, jax.random.fold_in(stream_key, 6)
    for axis_at, blocks in cuts:
        steps = jnp.exp(jax.random.uniform(jax.random.fold_in(own, axis_at), (blocks,), jnp.float32, least / len(cuts), top_value / len(cuts)))
        gain = gain * jnp.repeat(steps, shape[axis_at] // blocks).reshape([-1 if axis == axis_at else 1 for axis in range(len(shape))])
    return gain


def shared_out(own_key, own, number, rows, number_of, top, limit, skew):
    ranking = jax.random.permutation(own_key, number_of)
    heavy_load, common = shares(number_of, rows * top, limit, skew, True), shares(number_of, rows * top, limit, skew, False)
    places = jnp.arange(number_of)

    def named(lengths, rotation):
        used = int((lengths > 0).sum())
        fixed = max(1, used // 4)
        passed = fixed + (places - fixed + rotation * (used - fixed)) % max(1, number_of - fixed)
        return jnp.zeros((number_of,), jnp.int32).at[ranking[jnp.where(places < fixed, places, passed)]].set(jnp.asarray(lengths, jnp.int32))

    lengths = jnp.where(number % 4 == 0, named(heavy_load, number // 4), named(common, number - number // 4 - 1))
    mixed = jax.random.permutation(jax.random.fold_in(own, 3), number_of)
    giver, taker = mixed[0:number_of // 2 * 2:2], mixed[1:number_of // 2 * 2:2]
    margin = jnp.minimum(lengths[giver] - 1, limit - lengths[taker]) // 2
    margin = jnp.where((giver == ranking[0]) | (taker == ranking[0]) | (lengths[taker] == 0), 0, jnp.maximum(margin, 0))
    passed = jax.random.randint(jax.random.fold_in(own, 4), (number_of // 2,), 0, 1 << 20) % (margin + 1)
    lengths = lengths.at[giver].add(-passed).at[taker].add(passed)
    members = jnp.searchsorted(jnp.cumsum(lengths), jnp.arange(rows * top), side="right").astype(jnp.int32)
    grid = members.reshape(top, rows).T
    grid = grid[jax.random.permutation(jax.random.fold_in(own, 1), rows)]
    rotation = jax.random.randint(jax.random.fold_in(own, 2), (rows, 1), 0, top)
    return jnp.take_along_axis(grid, (jnp.arange(top)[None, :] + rotation) % top, axis=1)


def shares(amount, total, reach, skew, full):
    loads = [(1 << 20) // math.isqrt(rank ** skew) + 1 for rank in range(1, amount + 1)]
    largest = reach if full else min(reach, max(-(-total // amount), total * loads[0] // sum(loads)))
    least = 1 if total - largest >= amount - 1 else 0
    given, rest = [largest] + [least] * (amount - 1), total - largest - least * (amount - 1)
    while rest > 0:
        free = [i for i in range(1, amount) if given[i] < largest] or [i for i in range(1, amount) if given[i] < reach]
        whole, budget = sum([loads[i] for i in free]), rest
        for i in free:
            addition = min(reach - given[i], max(1, budget * loads[i] // whole), rest)
            given[i] = given[i] + addition
            rest = rest - addition
    return np.array(given)


def centred(key, dims, width, bound, shards=(), held_as=jnp.bfloat16):
    level = block_scale(key, dims, shards, -0.22, 0.18) if shards else 1.0
    array = jax.random.normal(key, dims, jnp.float32) * width * level
    return jnp.minimum(jnp.maximum(array, -bound), bound).astype(held_as)


def setup_inputs(seed: int = 0) -> dict:
    key_of = jax.random.split(jax.random.key(seed), 8)
    tokens = centred(key_of[0], (TOKENS, D), 1.0, 6.0, ((0, 32),))
    route_weight = jnp.clip(jnp.exp(math.log(0.4) - 2.5902672 * jax.random.uniform(key_of[1], (TOKENS, TOPK), jnp.float32) ** block_scale(key_of[1], (TOKENS, TOPK), ((0, 32),), -0.2, 0.2)), 0.03, 0.4)
    upstream = centred(key_of[2], (TOKENS, D), 1.0, 6.0, ((0, 32),))
    expert_index_keys = jax.random.split(jax.random.fold_in(key_of[3], 1), TOKENS // TOK_DEV)
    expert_index_turns = jax.random.permutation(jax.random.fold_in(key_of[3], 3), TOKENS // TOK_DEV)
    expert_index = jax.vmap(lambda own, number: shared_out(jax.random.fold_in(key_of[3], 2), own, number, TOK_DEV, EXPERTS, TOPK, CAP, 2))(expert_index_keys, expert_index_turns).reshape((TOKENS, TOPK))
    gate_weight = centred(key_of[4], (EXPERTS, D, FF), D ** -0.5, 0.125, ((0, 16), (1, 2)))
    up_weight = centred(key_of[5], (EXPERTS, D, FF), D ** -0.5, 0.125, ((0, 16), (1, 2)))
    down_weight = centred(key_of[6], (EXPERTS, D, FF), FF ** -0.5, 0.21875, ((0, 16), (1, 2)))
    return {"tokens": tokens, "route_weight": route_weight, "upstream": upstream, "expert_index": expert_index, "gate_weight": gate_weight, "up_weight": up_weight, "down_weight": down_weight}


def silu_parts(gate_value):
    sigmoid_value = jax.nn.sigmoid(gate_value)
    return gate_value * sigmoid_value, sigmoid_value * (1.0 + gate_value * (1.0 - sigmoid_value))


def contract_last(left, right):
    return lax.dot_general(left, right, (((1,), (1,)), ((), ())), preferred_element_type=jnp.float32)


def slot_table(expert_index):
    devices_all = N_DP * N_EXPERT
    assignments = TOK_DEV * TOPK
    flat_ids = expert_index.reshape(devices_all, assignments).astype(jnp.int32)
    onehot = (flat_ids[:, :, None] == jnp.arange(EXPERTS, dtype=jnp.int32)[None, None, :]).astype(jnp.int32)
    earlier = jnp.cumsum(onehot, axis=1) - onehot
    slot_value = jnp.sum(earlier * onehot, axis=2).astype(jnp.int32)
    device_of = jnp.broadcast_to(jnp.arange(devices_all, dtype=jnp.int32)[:, None], (devices_all, assignments))
    flat_place = (device_of * assignments + jnp.arange(assignments, dtype=jnp.int32)[None, :]).astype(jnp.int32)
    slot_grid = jnp.full((EXPERTS, devices_all, CAP), -1, jnp.int32)
    slot_grid = slot_grid.at[flat_ids, device_of, slot_value].set(flat_place)
    return slot_grid.reshape(EXPERTS, devices_all * CAP)


def reference(tokens, route_weight, upstream, expert_index, gate_weight, up_weight, down_weight):
    slot_grid = slot_table(expert_index)
    flat_route = route_weight.reshape(-1)
    row_total = N_EXPERT * CAP

    def per_expert(running, inputs):
        out_sum, grad_sum, route_sum = running
        slot_index, w_gate, w_up, w_down = inputs
        filled = slot_index >= 0
        safe_index = jnp.maximum(slot_index, 0).astype(jnp.int32)
        token_of = (safe_index // TOPK).astype(jnp.int32)
        routed_tokens = jnp.where(filled[:, None], tokens[token_of], jnp.zeros((), jnp.bfloat16))
        weight_of = jnp.where(filled, flat_route[safe_index], jnp.float32(0.0))
        upstream_rows = upstream[token_of].astype(jnp.float32)
        routed_grads = jnp.where(filled[:, None], weight_of[:, None] * upstream_rows, jnp.float32(0.0)).astype(jnp.bfloat16)
        gate_value = jnp.dot(routed_tokens, w_gate, preferred_element_type=jnp.float32)
        up_value = jnp.dot(routed_tokens, w_up, preferred_element_type=jnp.float32)
        activated, slope_value = silu_parts(gate_value)
        hidden = (activated * up_value).astype(jnp.bfloat16)
        expert_out = contract_last(hidden, w_down).astype(jnp.bfloat16)
        out_float = expert_out.astype(jnp.float32)
        out_sum = out_sum.at[token_of].add(jnp.where(filled[:, None], weight_of[:, None] * out_float, jnp.float32(0.0)))
        route_terms = jnp.sum(out_float * upstream_rows, axis=1)
        route_sum = route_sum.at[safe_index].add(jnp.where(filled, route_terms, jnp.float32(0.0)))
        hidden_grad = jnp.dot(routed_grads, w_down, preferred_element_type=jnp.float32)
        gate_grad = (hidden_grad * up_value * slope_value).astype(jnp.bfloat16)
        up_grad = (hidden_grad * activated).astype(jnp.bfloat16)
        row_grad = (contract_last(gate_grad, w_gate) + contract_last(up_grad, w_up)).astype(jnp.bfloat16)
        grad_sum = grad_sum.at[token_of].add(jnp.where(filled[:, None], row_grad.astype(jnp.float32), jnp.float32(0.0)))
        grads_group = routed_grads.reshape(N_DP, row_total, D).astype(jnp.float32)
        hidden_group = hidden.reshape(N_DP, row_total, FF).astype(jnp.float32)
        group_part = jnp.einsum("grd,grf->gdf", grads_group, hidden_group).astype(jnp.bfloat16)
        group_part = lax.optimization_barrier(group_part)
        down_grad = jnp.sum(group_part.astype(jnp.float32), axis=0).astype(jnp.bfloat16)
        return (out_sum, grad_sum, route_sum), down_grad

    initial = (jnp.zeros((TOKENS, D), jnp.float32), jnp.zeros((TOKENS, D), jnp.float32), jnp.zeros((TOKENS * TOPK,), jnp.float32))
    finals, down_grad = lax.scan(per_expert, initial, (slot_grid, gate_weight, up_weight, down_weight))
    out_sum, grad_sum, route_sum = finals
    return out_sum.astype(jnp.bfloat16), grad_sum.astype(jnp.bfloat16), route_sum.reshape(TOKENS, TOPK), down_grad
```

```python
import functools

import jax
import jax.numpy as jnp
from jax import lax
from jax.experimental import pallas as pl
from jax.experimental.pallas import tpu as pltpu
from jax.sharding import PartitionSpec as P

BF16 = jnp.bfloat16
F32 = jnp.float32
LANES = 128
CORE, SIDE = 2, 2
VMEM = pl.BlockSpec(memory_space=pltpu.VMEM)
SMEM = pl.BlockSpec(memory_space=pltpu.SMEM)
PARAMS = pltpu.CompilerParams(vmem_limit_bytes=32 * 1024 * 1024)


def dot_of(left, right, left_dim, right_dim):
    return lax.dot_general(
        left, right, (((left_dim,), (right_dim,)), ((), ())), preferred_element_type=F32
    )


def call(body, out_shapes, args, flops=0):
    moved = sum(a.size * a.dtype.itemsize for a in args)
    return pl.pallas_call(
        body,
        out_shape=[jax.ShapeDtypeStruct(s, t) for s, t in out_shapes],
        in_specs=[SMEM] + [VMEM] * (len(args) - 1),
        out_specs=[VMEM] * len(out_shapes),
        compiler_params=PARAMS,
        cost_estimate=pl.CostEstimate(flops=flops, bytes_accessed=moved, transcendentals=0),
    )(*args)


def pack_kernel(n_dp, n_experts, half, ids, tok_ref, up_ref, rw_ref, idx_ref, *outs):
    rows, top = idx_ref.shape
    extra = outs[0].shape[1] - 2 * half
    lane = lax.broadcasted_iota(jnp.int32, (rows, extra), 1)
    high_at, low_at = jnp.zeros((rows, extra), F32), jnp.zeros((rows, extra), F32)
    for k in range(top):
        named = idx_ref[:, k : k + 1]
        weight = rw_ref[:, k : k + 1]
        high_at = jnp.where(lane == named, weight, high_at)
        low_at = jnp.where(lane == named + n_experts, weight, low_at)
    low_at = low_at - low_at.astype(BF16).astype(F32)
    routing = (high_at + low_at).astype(BF16)
    for s, out in enumerate(outs):
        owner = lax.rem(ids[0] + s, n_dp)
        at = pl.ds(pl.multiple_of(owner * half, LANES), half)
        out[:, :half] = tok_ref[:, at]
        out[:, half : 2 * half] = up_ref[:, at]
        out[:, 2 * half :] = routing


def forward_kernel(n_dp, n_experts, tok, cap, ids, near, side, core, wg, wu, wd, part, up_rows, sel, weight):
    half, ff = wg.shape
    data = jnp.concatenate([near[...], side[...], core[...]], axis=0)
    total, rows = data.shape[0], sel.shape[0]
    routing = data[:, 2 * half :]
    lane = lax.broadcasted_iota(jnp.int32, (8, routing.shape[1]), 1)
    pick = jnp.where((lane == ids[1]) | (lane == ids[1] + n_experts), 1.0, 0.0).astype(BF16)
    w_row = dot_of(pick, routing, 1, 1)
    chosen = w_row > 0.0
    before = lax.broadcasted_iota(jnp.int32, (total, total), 0)
    after = lax.broadcasted_iota(jnp.int32, (total, total), 1)
    earlier = jnp.where((before < after) & (before // tok == after // tok), 1.0, 0.0).astype(BF16)
    slot = dot_of(jnp.where(chosen, 1.0, 0.0).astype(BF16), earlier, 1, 0)
    block = lax.broadcasted_iota(jnp.int32, (8, total), 1) // tok
    shift = block % n_dp
    source = ids[0] - shift
    source = jnp.where(source < 0, source + n_dp, source)
    place = jnp.where(chosen, slot.astype(jnp.int32) + cap * (block - shift + source), -1)
    picked = lax.broadcasted_iota(jnp.int32, (rows, total), 0) == place[:1]
    chooser = jnp.where(picked, 1.0, 0.0).astype(BF16)
    sel[...] = chooser
    w_col = jnp.sum(jnp.where(picked, w_row[:1], 0.0), axis=1, keepdims=True)
    weight[...] = jnp.broadcast_to(w_col, weight.shape)
    tok_rows = dot_of(chooser, data[:, :half], 1, 0).astype(BF16)
    grad_rows = dot_of(chooser, data[:, half : 2 * half], 1, 0).astype(BF16)
    up_rows[...] = grad_rows
    part[:, :ff] = dot_of(tok_rows, wg[...], 1, 0).astype(BF16)
    part[:, ff : 2 * ff] = dot_of(tok_rows, wu[...], 1, 0).astype(BF16)
    part[:, 2 * ff :] = dot_of(grad_rows, wd[...], 1, 0).astype(BF16)


def backward_kernel(n_experts, n_parts, ids, *refs):
    parts = refs[:n_parts]
    sel, weight, wg, wu, wd, keep, send, hidden_rows = refs[n_parts:]
    half, ff = wg.shape
    whole = parts[0][...].astype(F32)
    for other in parts[1:]:
        whole = whole + other[...].astype(F32)
    gate, up, grad = whole[:, :ff], whole[:, ff : 2 * ff], whole[:, 2 * ff :]
    w_col = weight[:, :1]
    sig = 1.0 / (1.0 + jnp.exp(-gate))
    act = gate * sig
    hidden = act * up
    route = jnp.sum(hidden * grad, axis=1, keepdims=True)
    grad = grad * w_col
    weighted = (hidden * w_col).astype(BF16)
    hidden_rows[...] = weighted
    gate_grad = (grad * up * (sig * (1.0 + gate * (1.0 - sig)))).astype(BF16)
    up_grad = (grad * act).astype(BF16)
    lane = lax.broadcasted_iota(jnp.int32, (whole.shape[0], keep.shape[1] - 2 * half), 1)
    high = route.astype(BF16).astype(F32)
    columns = jnp.where(lane == ids[1], high, jnp.where(lane == ids[1] + n_experts, route - high, 0.0))
    spread = jnp.concatenate([weighted, gate_grad, up_grad, columns.astype(BF16)], axis=1)
    spread = dot_of(sel[...], spread, 0, 0).astype(BF16)
    out = dot_of(spread[:, :ff], wd[...], 1, 1)
    back = dot_of(spread[:, ff : 2 * ff], wg[...], 1, 1)
    back = back + dot_of(spread[:, 2 * ff : 3 * ff], wu[...], 1, 1)
    tops = keep.shape[0]
    for ref, rows in ((keep, slice(0, tops)), (send, slice(tops, 2 * tops))):
        ref[:, :half] = out[rows].astype(BF16)
        ref[:, half : 2 * half] = back[rows].astype(BF16)
        ref[:, 2 * half :] = spread[rows, 3 * ff :]


def down_kernel(chunks, ids, *refs):
    up_rows = jnp.concatenate([r[...] for r in refs[:chunks]], axis=0)
    hidden = jnp.concatenate([r[...] for r in refs[chunks : 2 * chunks]], axis=0)
    refs[2 * chunks][...] = dot_of(up_rows, hidden, 0, 0).astype(BF16)


def final_kernel(n_dp, n_experts, half, ids, own, idx_ref, *refs):
    others, (comb, grad, route) = refs[: n_dp - 1], refs[n_dp - 1 :]
    for s in range(n_dp):
        owner = lax.rem(ids[0] + s, n_dp)
        at = pl.ds(pl.multiple_of(owner * half, LANES), half)
        source = own if s == 0 else others[s - 1]
        comb[:, at] = source[:, :half]
        grad[:, at] = source[:, half : 2 * half]
    columns = own[:, 2 * half :].astype(F32)
    lane = lax.broadcasted_iota(jnp.int32, columns.shape, 1)
    rows, top = route.shape
    slot = lax.broadcasted_iota(jnp.int32, (rows, top), 1)
    result = jnp.zeros((rows, top), F32)
    for k in range(top):
        named = idx_ref[:, k : k + 1]
        mine = (lane == named) | (lane == named + n_experts)
        value = jnp.sum(jnp.where(mine, columns, 0.0), axis=1, keepdims=True)
        result = jnp.where(slot == k, value, result)
    route[...] = result


def added(left, right):
    return (left.astype(F32) + right.astype(F32)).astype(BF16)


def on_device(tokens, route_weight, upstream, expert_index, gate_weight, up_weight, down_weight):
    n_experts, n_dp = lax.axis_size("expert"), lax.axis_size("dp")
    tok, top = expert_index.shape
    width = tokens.shape[1]
    wg, wu, wd = gate_weight[0], up_weight[0], down_weight[0]
    half, ff = wg.shape
    cap = max(2, (5 * tok * top + 4 * n_experts - 1) // (4 * n_experts))
    extra = -(-2 * n_experts // LANES) * LANES
    layers = n_experts // (SIDE * CORE)
    wide = 2 * half + extra
    group = n_dp * tok
    rows = CORE * SIDE * n_dp * cap
    total = CORE * SIDE * group
    ids = jnp.stack([lax.axis_index("dp"), lax.axis_index("expert")]).astype(jnp.int32)

    def dp_shift(x, s):
        return lax.ppermute(x, "dp", [(i, (i + s) % n_dp) for i in range(n_dp)])

    def layer_shift(x, k):
        step = SIDE * CORE * k
        return lax.ppermute(x, "expert", [(i, (i + step) % n_experts) for i in range(n_experts)])

    def swap(x, bit):
        return lax.ppermute(x, "expert", [(i, i ^ bit) for i in range(n_experts)])

    blocks = call(
        functools.partial(pack_kernel, n_dp, n_experts, half),
        [((tok, wide), BF16)] * n_dp,
        (ids, tokens, upstream, route_weight, expert_index),
    )
    mine = jnp.concatenate([blocks[0]] + [dp_shift(blocks[s], s) for s in range(1, n_dp)], axis=0)

    order = [0]
    for k in range(1, layers // 2 + 1):
        order += [k] if 2 * k == layers else [k, layers - k]
    order = order[:layers]

    near = {k: mine if k == 0 else layer_shift(mine, k) for k in order}
    parts, kept = {}, {}
    for k in order:
        side = swap(near[k], CORE)
        core = swap(jnp.concatenate([near[k], side], axis=0), 1)
        part, up_rows, sel, weight = call(
            functools.partial(forward_kernel, n_dp, n_experts, tok, cap),
            [
                ((rows, 3 * ff), BF16),
                ((rows, half), BF16),
                ((rows, total), BF16),
                ((rows, LANES), F32),
            ],
            (ids, near[k], side, core, wg, wu, wd),
            flops=2 * rows * half * 3 * ff + 4 * rows * total * half,
        )
        parts[k] = [part] + [dp_shift(part, s) for s in range(1, n_dp)]
        kept[k] = (up_rows, sel, weight)

    hidden_rows, sums = {}, {}
    for k in order:
        up_rows, sel, weight = kept[k]
        keep, send, hidden_rows[k] = call(
            functools.partial(backward_kernel, n_experts, n_dp),
            [((total // 2, wide), BF16), ((total // 2, wide), BF16), ((rows, ff), BF16)],
            (ids, *parts[k], sel, weight, wg, wu, wd),
            flops=2 * total * half * 3 * ff + 2 * rows * total * 3 * ff,
        )
        back = swap(send, 1)
        outward = swap(added(keep[group:], back[group:]), CORE)
        partial = added(added(keep[:group], back[:group]), outward)
        sums[k] = partial if k == 0 else layer_shift(partial, -k)

    (down_grad,) = call(
        functools.partial(down_kernel, layers),
        [((half, ff), BF16)],
        (ids, *[kept[k][0] for k in order], *[hidden_rows[k] for k in order]),
        flops=2 * layers * rows * half * ff,
    )
    result = sums[0].astype(F32)
    for k in order[1:]:
        result = result + sums[k].astype(F32)
    result = result.astype(BF16)
    others = [dp_shift(result[s * tok : (s + 1) * tok, : 2 * half], -s) for s in range(1, n_dp)]
    combined, token_grad, route_grad = call(
        functools.partial(final_kernel, n_dp, n_experts, half),
        [((tok, width), BF16), ((tok, width), BF16), ((tok, top), F32)],
        (ids, result[:tok], expert_index, *others),
    )
    return (combined, token_grad, route_grad, down_grad[None])


def solution(mesh):
    return jax.shard_map(
        on_device,
        mesh=mesh,
        in_specs=(
            P(("dp", "expert"), None),
            P(("dp", "expert"), None),
            P(("dp", "expert"), None),
            P(("dp", "expert"), None),
            P("expert", "dp", None),
            P("expert", "dp", None),
            P("expert", "dp", None),
        ),
        out_specs=(
            P(("dp", "expert"), None),
            P(("dp", "expert"), None),
            P(("dp", "expert"), None),
            P("expert", "dp", None),
        ),
        check_vma=False,
    )
```

```python
import functools

import jax
import jax.numpy as jnp
from jax import lax
from jax.experimental import pallas as pl
from jax.experimental.pallas import tpu as pltpu
from jax.sharding import PartitionSpec as P

BF16 = jnp.bfloat16
F32 = jnp.float32
LANES = 128
CORE, SIDE = 2, 2
PIECE_ROWS, PIECE_COLS = 2, 2
PIECES = PIECE_ROWS * PIECE_COLS
WINDOW = 2
VMEM = pl.BlockSpec(memory_space=pltpu.VMEM)
SMEM = pl.BlockSpec(memory_space=pltpu.SMEM)
PARAMS = pltpu.CompilerParams(vmem_limit_bytes=32 * 1024 * 1024)
WIDE = pltpu.CompilerParams(vmem_limit_bytes=60 * 1024 * 1024)


def dot_of(left, right, left_dim, right_dim):
    return lax.dot_general(
        left, right, (((left_dim,), (right_dim,)), ((), ())), preferred_element_type=F32
    )


def call(body, out_shapes, args, far=(), copies=0, flops=0, params=PARAMS):
    moved = sum(a.size * a.dtype.itemsize for a in (*args, *far))
    return pl.pallas_call(
        body,
        out_shape=[jax.ShapeDtypeStruct(s, t) for s, t in out_shapes],
        in_specs=[SMEM] + [VMEM] * (len(args) - 1) + [pl.BlockSpec(memory_space=pltpu.HBM)] * len(far),
        out_specs=[VMEM] * len(out_shapes),
        scratch_shapes=[pltpu.SemaphoreType.DMA((copies,))] if copies else [],
        compiler_params=params,
        cost_estimate=pl.CostEstimate(flops=flops, bytes_accessed=moved, transcendentals=0),
    )(*args, *far)


def pack_kernel(n_dp, n_experts, half, ids, rw_ref, idx_ref, tok_ref, up_ref, *refs):
    outs, sem = refs[:-1], refs[-1]
    copies = []
    for s, out in enumerate(outs):
        owner = lax.rem(ids[0] + s, n_dp)
        at = pl.ds(pl.multiple_of(owner * half, LANES), half)
        for which, source in enumerate((tok_ref, up_ref)):
            target = out.at[:, which * half : (which + 1) * half]
            copies.append(pltpu.make_async_copy(source.at[:, at], target, sem.at[2 * s + which]))
    for copy in copies:
        copy.start()
    top, rows = idx_ref.shape
    extra = outs[0].shape[1] - 2 * half
    lane = lax.broadcasted_iota(jnp.int32, (extra, rows), 0)
    high_at, low_at = jnp.zeros((extra, rows), F32), jnp.zeros((extra, rows), F32)
    for k in range(top):
        named = idx_ref[k : k + 1, :]
        weight = rw_ref[k : k + 1, :]
        high_at = jnp.where(lane == named, weight, high_at)
        low_at = jnp.where(lane == named + n_experts, weight, low_at)
    low_at = low_at - low_at.astype(BF16).astype(F32)
    same = lax.broadcasted_iota(jnp.int32, (extra, extra), 0) == lax.broadcasted_iota(jnp.int32, (extra, extra), 1)
    turned = dot_of((high_at + low_at).astype(BF16), jnp.where(same, 1.0, 0.0).astype(BF16), 0, 0)
    for out in outs:
        out[:, 2 * half :] = turned.astype(BF16)
    for copy in copies:
        copy.wait()


def load_kernel(ids, *refs):
    sources, outs, sem = refs[:3], refs[3:6], refs[6]
    copies = [pltpu.make_async_copy(source, out, sem.at[i]) for i, (source, out) in enumerate(zip(sources, outs))]
    for copy in copies:
        copy.start()
    for copy in copies:
        copy.wait()


def forward_kernel(n_dp, n_experts, tok, cap, ids, near, side, core, wg, wu, wd, *outs):
    *pieces, up_rows, sel, weight = outs
    half, ff = wg.shape
    data = jnp.concatenate([near[...], side[...], core[...]], axis=0)
    total, rows = data.shape[0], sel.shape[0]
    routing = data[:, 2 * half :]
    lane = lax.broadcasted_iota(jnp.int32, (8, routing.shape[1]), 1)
    pick = jnp.where((lane == ids[1]) | (lane == ids[1] + n_experts), 1.0, 0.0).astype(BF16)
    w_row = dot_of(pick, routing, 1, 1)
    chosen = w_row > 0.0
    before = lax.broadcasted_iota(jnp.int32, (total, total), 0)
    after = lax.broadcasted_iota(jnp.int32, (total, total), 1)
    earlier = jnp.where((before < after) & (before // tok == after // tok), 1.0, 0.0).astype(BF16)
    slot = dot_of(jnp.where(chosen, 1.0, 0.0).astype(BF16), earlier, 1, 0)
    block = lax.broadcasted_iota(jnp.int32, (8, total), 1) // tok
    shift = block % n_dp
    source = ids[0] - shift
    source = jnp.where(source < 0, source + n_dp, source)
    place = jnp.where(chosen, slot.astype(jnp.int32) + cap * (block - shift + source), -1)
    picked = lax.broadcasted_iota(jnp.int32, (rows, total), 0) == place[:1]
    chooser = jnp.where(picked, 1.0, 0.0).astype(BF16)
    sel[...] = chooser
    w_col = jnp.sum(jnp.where(picked, w_row[:1], 0.0), axis=1, keepdims=True)
    weight[...] = jnp.broadcast_to(w_col, weight.shape)
    tok_rows = dot_of(chooser, data[:, :half], 1, 0).astype(BF16)
    grad_rows = dot_of(chooser, data[:, half : 2 * half], 1, 0).astype(BF16)
    up_rows[...] = grad_rows
    sums = [
        dot_of(left, right[...], 1, 0).astype(BF16)
        for left, right in ((tok_rows, wg), (tok_rows, wu), (grad_rows, wd))
    ]
    part = jnp.concatenate(sums, axis=1)
    deep, wide = pieces[0].shape
    for at, piece in enumerate(pieces):
        r, c = divmod(at, 3 * ff // wide)
        piece[...] = part[r * deep : (r + 1) * deep, c * wide : (c + 1) * wide]


def backward_kernel(n_experts, n_parts, ids, *refs):
    sel, weight, wg, wu, wd, keep, send, hidden_rows = refs[PIECES * n_parts :]
    half, ff = wg.shape
    pieces = [sum(ref[...].astype(F32) for ref in refs[at * n_parts : (at + 1) * n_parts]) for at in range(PIECES)]
    whole = jnp.concatenate(
        [jnp.concatenate(pieces[at : at + PIECE_COLS], axis=1) for at in range(0, PIECES, PIECE_COLS)], axis=0
    )
    gate, up, grad = whole[:, :ff], whole[:, ff : 2 * ff], whole[:, 2 * ff :]
    w_col = weight[:, :1]
    sig = 1.0 / (1.0 + jnp.exp(-gate))
    act = gate * sig
    hidden = act * up
    route = jnp.sum(hidden * grad, axis=1, keepdims=True)
    grad = grad * w_col
    weighted = (hidden * w_col).astype(BF16)
    hidden_rows[...] = weighted
    gate_grad = (grad * up * (sig * (1.0 + gate * (1.0 - sig)))).astype(BF16)
    up_grad = (grad * act).astype(BF16)
    lane = lax.broadcasted_iota(jnp.int32, (whole.shape[0], keep.shape[1] - 2 * half), 1)
    high = route.astype(BF16).astype(F32)
    columns = jnp.where(lane == ids[1], high, jnp.where(lane == ids[1] + n_experts, route - high, 0.0))
    spread = jnp.concatenate([weighted, gate_grad, up_grad, columns.astype(BF16)], axis=1)
    spread = dot_of(sel[...], spread, 0, 0).astype(BF16)
    out = dot_of(spread[:, :ff], wd[...], 1, 1)
    back = dot_of(spread[:, ff : 2 * ff], wg[...], 1, 1)
    back = back + dot_of(spread[:, 2 * ff : 3 * ff], wu[...], 1, 1)
    tops = keep.shape[0]
    for ref, rows in ((keep, slice(0, tops)), (send, slice(tops, 2 * tops))):
        ref[:, :half] = out[rows].astype(BF16)
        ref[:, half : 2 * half] = back[rows].astype(BF16)
        ref[:, 2 * half :] = spread[rows, 3 * ff :]


def down_kernel(chunks, ids, *refs):
    up_rows = jnp.concatenate([r[...] for r in refs[:chunks]], axis=0)
    hidden = jnp.concatenate([r[...] for r in refs[chunks : 2 * chunks]], axis=0)
    refs[2 * chunks][...] = dot_of(up_rows, hidden, 0, 0).astype(BF16)


def final_kernel(n_dp, n_experts, half, ids, own, idx_ref, *refs):
    others, (comb, grad, route) = refs[: n_dp - 1], refs[n_dp - 1 :]
    for s in range(n_dp):
        owner = lax.rem(ids[0] + s, n_dp)
        at = pl.ds(pl.multiple_of(owner * half, LANES), half)
        source = own if s == 0 else others[s - 1]
        comb[:, at] = source[:, :half]
        grad[:, at] = source[:, half : 2 * half]
    columns = own[:, 2 * half :]
    extra = columns.shape[1]
    same = lax.broadcasted_iota(jnp.int32, (extra, extra), 0) == lax.broadcasted_iota(jnp.int32, (extra, extra), 1)
    turned = dot_of(jnp.where(same, 1.0, 0.0).astype(BF16), columns, 1, 1)
    lane = lax.broadcasted_iota(jnp.int32, turned.shape, 0)
    top = route.shape[0]
    for k in range(top):
        named = idx_ref[k : k + 1, :]
        mine = (lane == named) | (lane == named + n_experts)
        route[k : k + 1, :] = jnp.sum(jnp.where(mine, turned, 0.0), axis=0, keepdims=True)


def after(x, *earlier):
    return lax.optimization_barrier((x, *earlier))[0]


def added(left, right):
    return (left.astype(F32) + right.astype(F32)).astype(BF16)


def on_device(tokens, route_weight, upstream, expert_index, gate_weight, up_weight, down_weight):
    n_experts, n_dp = lax.axis_size("expert"), lax.axis_size("dp")
    tok, top = expert_index.shape
    width = tokens.shape[1]
    wg, wu, wd = gate_weight[0], up_weight[0], down_weight[0]
    half, ff = wg.shape
    cap = max(2, (5 * tok * top + 4 * n_experts - 1) // (4 * n_experts))
    extra = -(-2 * n_experts // LANES) * LANES
    layers = n_experts // (SIDE * CORE)
    wide = 2 * half + extra
    group = n_dp * tok
    rows = CORE * SIDE * n_dp * cap
    total = CORE * SIDE * group
    ids = jnp.stack([lax.axis_index("dp"), lax.axis_index("expert")]).astype(jnp.int32)

    def dp_shift(x, s):
        return lax.ppermute(x, "dp", [(i, (i + s) % n_dp) for i in range(n_dp)])

    def layer_shift(x, k):
        step = SIDE * CORE * k
        return lax.ppermute(x, "expert", [(i, (i + step) % n_experts) for i in range(n_experts)])

    def swap(x, bit):
        return lax.ppermute(x, "expert", [(i, i ^ bit) for i in range(n_experts)])

    index_rows = expert_index.T
    blocks = call(
        functools.partial(pack_kernel, n_dp, n_experts, half),
        [((tok, wide), BF16)] * n_dp,
        (ids, route_weight.T, index_rows),
        far=(tokens, upstream),
        copies=2 * n_dp,
        params=WIDE,
    )
    mine = jnp.concatenate([blocks[0]] + [dp_shift(blocks[s], s) for s in range(1, n_dp)], axis=0)
    wg, wu, wd = call(load_kernel, [((half, ff), BF16)] * 3, (ids,), far=(wg, wu, wd), copies=3)

    near, sides, parts, kept, crossed = [mine], [], [], [], []
    hidden_rows, partials, homes = [], [], []
    order = [k for k in (0, 2, 1, 3) if k < layers] + list(range(4, layers))

    def over_dp(part):
        if len(crossed) >= WINDOW:
            part = after(part, crossed[-WINDOW])
        others = [dp_shift(part, s) for s in range(1, n_dp)]
        crossed.extend(others[-1:])
        return [part] + others

    def forward(i):
        sides.append(swap(near[i], CORE))
        both = jnp.concatenate([near[i], sides[i]], axis=0)
        if i + 1 < layers:
            near.append(layer_shift(after(mine, near[i]) if i else mine, order[i + 1]))
        if i == 0:
            both = after(both, wg, wu, wd)
        core = swap(both, 1)
        *pieces, up_rows, sel, weight = call(
            functools.partial(forward_kernel, n_dp, n_experts, tok, cap),
            [
                *[((rows // PIECE_ROWS, 3 * ff // PIECE_COLS), BF16)] * PIECES,
                ((rows, half), BF16),
                ((rows, total), BF16),
                ((rows, LANES), F32),
            ],
            (ids, near[i], sides[i], core, wg, wu, wd),
            flops=2 * rows * half * 3 * ff + 4 * rows * total * half,
        )
        kept.append((up_rows, sel, weight))
        if i >= 3:
            pieces = [after(piece, partials[i - 3]) for piece in pieces]
        parts.append(sum([over_dp(piece) for piece in pieces], []))

    def backward(i):
        up_rows, sel, weight = kept[i]
        keep, send, hidden = call(
            functools.partial(backward_kernel, n_experts, n_dp),
            [((total // 2, wide), BF16), ((total // 2, wide), BF16), ((rows, ff), BF16)],
            (ids, *parts[i], sel, weight, wg, wu, wd),
            flops=2 * total * half * 3 * ff + 2 * rows * total * 3 * ff,
        )
        hidden_rows.append(hidden)
        back = swap(send, 1)
        outward = swap(added(keep[group:], back[group:]), CORE)
        partials.append(added(added(keep[:group], back[:group]), outward))
        homes.append(layer_shift(partials[i], -order[i]) if order[i] else partials[i])

    for i in range(layers + 2):
        if i >= 2:
            backward(i - 2)
        if i < layers:
            forward(i)

    (down_grad,) = call(
        functools.partial(down_kernel, layers),
        [((half, ff), BF16)],
        (ids, *[rows_of[0] for rows_of in kept], *hidden_rows),
        flops=2 * layers * rows * half * ff,
    )
    result = sum(partial.astype(F32) for partial in homes)
    result = result.astype(BF16)
    others = [dp_shift(result[s * tok : (s + 1) * tok, : 2 * half], -s) for s in range(1, n_dp)]
    combined, token_grad, route_grad = call(
        functools.partial(final_kernel, n_dp, n_experts, half),
        [((tok, width), BF16), ((tok, width), BF16), ((top, tok), F32)],
        (ids, result[:tok], index_rows, *others),
    )
    return (combined, token_grad, route_grad.T, down_grad[None])


def solution(mesh):
    return jax.shard_map(
        on_device,
        mesh=mesh,
        in_specs=(
            P(("dp", "expert"), None),
            P(("dp", "expert"), None),
            P(("dp", "expert"), None),
            P(("dp", "expert"), None),
            P("expert", "dp", None),
            P("expert", "dp", None),
            P("expert", "dp", None),
        ),
        out_specs=(
            P(("dp", "expert"), None),
            P(("dp", "expert"), None),
            P(("dp", "expert"), None),
            P("expert", "dp", None),
        ),
        check_vma=False,
    )
```

```python
import functools

import jax
import jax.numpy as jnp
from jax import lax
from jax.experimental import pallas as pl
from jax.experimental.pallas import tpu as pltpu
from jax.sharding import PartitionSpec as P

BF16 = jnp.bfloat16
F32 = jnp.float32
LANES = 128
CORE, SIDE = 2, 2
PIECE_ROWS, PIECE_COLS = 2, 2
PIECES = PIECE_ROWS * PIECE_COLS
WINDOW = 2
VMEM = pl.BlockSpec(memory_space=pltpu.VMEM)
SMEM = pl.BlockSpec(memory_space=pltpu.SMEM)
PARAMS = pltpu.CompilerParams(vmem_limit_bytes=32 * 1024 * 1024)
WIDE = pltpu.CompilerParams(vmem_limit_bytes=60 * 1024 * 1024)


def dot_of(left, right, left_dim, right_dim):
    return lax.dot_general(
        left, right, (((left_dim,), (right_dim,)), ((), ())), preferred_element_type=F32
    )


def call(body, out_shapes, args, far=(), copies=0, flops=0, params=PARAMS):
    moved = sum(a.size * a.dtype.itemsize for a in (*args, *far))
    return pl.pallas_call(
        body,
        out_shape=[jax.ShapeDtypeStruct(s, t) for s, t in out_shapes],
        in_specs=[SMEM] + [VMEM] * (len(args) - 1) + [pl.BlockSpec(memory_space=pltpu.HBM)] * len(far),
        out_specs=[VMEM] * len(out_shapes),
        scratch_shapes=[pltpu.SemaphoreType.DMA((copies,))] if copies else [],
        compiler_params=params,
        cost_estimate=pl.CostEstimate(flops=flops, bytes_accessed=moved, transcendentals=0),
    )(*args, *far)


def pack_kernel(n_dp, n_experts, half, ids, rw_ref, idx_ref, tok_ref, up_ref, *refs):
    outs, sem = refs[:-1], refs[-1]
    copies = []
    for s, out in enumerate(outs):
        owner = lax.rem(ids[0] + s, n_dp)
        at = pl.ds(pl.multiple_of(owner * half, LANES), half)
        for which, source in enumerate((tok_ref, up_ref)):
            target = out.at[:, which * half : (which + 1) * half]
            copies.append(pltpu.make_async_copy(source.at[:, at], target, sem.at[2 * s + which]))
    for copy in copies:
        copy.start()
    top, rows = idx_ref.shape
    extra = outs[0].shape[1] - 2 * half
    lane = lax.broadcasted_iota(jnp.int32, (extra, rows), 0)
    high_at, low_at = jnp.zeros((extra, rows), F32), jnp.zeros((extra, rows), F32)
    for k in range(top):
        named = idx_ref[k : k + 1, :]
        weight = rw_ref[k : k + 1, :]
        high_at = jnp.where(lane == named, weight, high_at)
        low_at = jnp.where(lane == named + n_experts, weight, low_at)
    low_at = low_at - low_at.astype(BF16).astype(F32)
    same = lax.broadcasted_iota(jnp.int32, (extra, extra), 0) == lax.broadcasted_iota(jnp.int32, (extra, extra), 1)
    turned = dot_of((high_at + low_at).astype(BF16), jnp.where(same, 1.0, 0.0).astype(BF16), 0, 0)
    for out in outs:
        out[:, 2 * half :] = turned.astype(BF16)
    for copy in copies:
        copy.wait()


def load_kernel(ids, *refs):
    sources, outs, sem = refs[:3], refs[3:6], refs[6]
    copies = [pltpu.make_async_copy(source, out, sem.at[i]) for i, (source, out) in enumerate(zip(sources, outs))]
    for copy in copies:
        copy.start()
    for copy in copies:
        copy.wait()


def forward_kernel(n_dp, n_experts, tok, cap, ids, near, side, core, wg, wu, wd, *outs):
    *pieces, up_rows, sel, weight = outs
    half, ff = wg.shape
    data = jnp.concatenate([near[...], side[...], core[...]], axis=0)
    total, rows = data.shape[0], sel.shape[0]
    routing = data[:, 2 * half :]
    lane = lax.broadcasted_iota(jnp.int32, (8, routing.shape[1]), 1)
    pick = jnp.where((lane == ids[1]) | (lane == ids[1] + n_experts), 1.0, 0.0).astype(BF16)
    w_row = dot_of(pick, routing, 1, 1)
    chosen = w_row > 0.0
    before = lax.broadcasted_iota(jnp.int32, (total, total), 0)
    after = lax.broadcasted_iota(jnp.int32, (total, total), 1)
    earlier = jnp.where((before < after) & (before // tok == after // tok), 1.0, 0.0).astype(BF16)
    slot = dot_of(jnp.where(chosen, 1.0, 0.0).astype(BF16), earlier, 1, 0)
    block = lax.broadcasted_iota(jnp.int32, (8, total), 1) // tok
    shift = block % n_dp
    source = ids[0] - shift
    source = jnp.where(source < 0, source + n_dp, source)
    place = jnp.where(chosen, slot.astype(jnp.int32) + cap * (block - shift + source), -1)
    picked = lax.broadcasted_iota(jnp.int32, (rows, total), 0) == place[:1]
    chooser = jnp.where(picked, 1.0, 0.0).astype(BF16)
    sel[...] = chooser
    w_col = jnp.sum(jnp.where(picked, w_row[:1], 0.0), axis=1, keepdims=True)
    weight[...] = jnp.broadcast_to(w_col, weight.shape)
    tok_rows = dot_of(chooser, data[:, :half], 1, 0).astype(BF16)
    grad_rows = dot_of(chooser, data[:, half : 2 * half], 1, 0).astype(BF16)
    up_rows[...] = grad_rows
    sums = [
        dot_of(left, right[...], 1, 0).astype(BF16)
        for left, right in ((tok_rows, wg), (tok_rows, wu), (grad_rows, wd))
    ]
    part = jnp.concatenate(sums, axis=1)
    deep, wide = pieces[0].shape
    for at, piece in enumerate(pieces):
        r, c = divmod(at, 3 * ff // wide)
        piece[...] = part[r * deep : (r + 1) * deep, c * wide : (c + 1) * wide]


def backward_kernel(n_experts, n_parts, ids, *refs):
    sel, weight, wg, wu, wd, keep, send, hidden_rows = refs[PIECES * n_parts :]
    half, ff = wg.shape
    pieces = [sum(ref[...].astype(F32) for ref in refs[at * n_parts : (at + 1) * n_parts]) for at in range(PIECES)]
    whole = jnp.concatenate(
        [jnp.concatenate(pieces[at : at + PIECE_COLS], axis=1) for at in range(0, PIECES, PIECE_COLS)], axis=0
    )
    gate, up, grad = whole[:, :ff], whole[:, ff : 2 * ff], whole[:, 2 * ff :]
    w_col = weight[:, :1]
    sig = 1.0 / (1.0 + jnp.exp(-gate))
    act = gate * sig
    hidden = act * up
    route = jnp.sum(hidden * grad, axis=1, keepdims=True)
    grad = grad * w_col
    weighted = (hidden * w_col).astype(BF16)
    hidden_rows[...] = weighted
    gate_grad = (grad * up * (sig * (1.0 + gate * (1.0 - sig)))).astype(BF16)
    up_grad = (grad * act).astype(BF16)
    lane = lax.broadcasted_iota(jnp.int32, (whole.shape[0], keep.shape[1] - 2 * half), 1)
    high = route.astype(BF16).astype(F32)
    columns = jnp.where(lane == ids[1], high, jnp.where(lane == ids[1] + n_experts, route - high, 0.0))
    spread = jnp.concatenate([weighted, gate_grad, up_grad, columns.astype(BF16)], axis=1)
    spread = dot_of(sel[...], spread, 0, 0).astype(BF16)
    out = dot_of(spread[:, :ff], wd[...], 1, 1)
    back = dot_of(spread[:, ff : 2 * ff], wg[...], 1, 1)
    back = back + dot_of(spread[:, 2 * ff : 3 * ff], wu[...], 1, 1)
    tops = keep.shape[0]
    for ref, rows in ((keep, slice(0, tops)), (send, slice(tops, 2 * tops))):
        ref[:, :half] = out[rows].astype(BF16)
        ref[:, half : 2 * half] = back[rows].astype(BF16)
        ref[:, 2 * half :] = spread[rows, 3 * ff :]


def down_kernel(chunks, ids, *refs):
    up_rows = jnp.concatenate([r[...] for r in refs[:chunks]], axis=0)
    hidden = jnp.concatenate([r[...] for r in refs[chunks : 2 * chunks]], axis=0)
    refs[2 * chunks][...] = dot_of(up_rows, hidden, 0, 0).astype(BF16)


def final_kernel(n_dp, n_experts, half, ids, own, idx_ref, *refs):
    others, (comb, grad, route) = refs[: n_dp - 1], refs[n_dp - 1 :]
    for s in range(n_dp):
        owner = lax.rem(ids[0] + s, n_dp)
        at = pl.ds(pl.multiple_of(owner * half, LANES), half)
        source = own if s == 0 else others[s - 1]
        comb[:, at] = source[:, :half]
        grad[:, at] = source[:, half : 2 * half]
    columns = own[:, 2 * half :]
    extra = columns.shape[1]
    same = lax.broadcasted_iota(jnp.int32, (extra, extra), 0) == lax.broadcasted_iota(jnp.int32, (extra, extra), 1)
    turned = dot_of(jnp.where(same, 1.0, 0.0).astype(BF16), columns, 1, 1)
    lane = lax.broadcasted_iota(jnp.int32, turned.shape, 0)
    top = route.shape[0]
    for k in range(top):
        named = idx_ref[k : k + 1, :]
        mine = (lane == named) | (lane == named + n_experts)
        route[k : k + 1, :] = jnp.sum(jnp.where(mine, turned, 0.0), axis=0, keepdims=True)


def after(x, *earlier):
    return lax.optimization_barrier((x, *earlier))[0]


def added(left, right):
    return (left.astype(F32) + right.astype(F32)).astype(BF16)


def on_device(tokens, route_weight, upstream, expert_index, gate_weight, up_weight, down_weight):
    n_experts, n_dp = lax.axis_size("expert"), lax.axis_size("dp")
    tok, top = expert_index.shape
    width = tokens.shape[1]
    wg, wu, wd = gate_weight[0], up_weight[0], down_weight[0]
    half, ff = wg.shape
    cap = max(2, (5 * tok * top + 4 * n_experts - 1) // (4 * n_experts))
    extra = -(-2 * n_experts // LANES) * LANES
    layers = n_experts // (SIDE * CORE)
    wide = 2 * half + extra
    group = n_dp * tok
    rows = CORE * SIDE * n_dp * cap
    total = CORE * SIDE * group
    ids = jnp.stack([lax.axis_index("dp"), lax.axis_index("expert")]).astype(jnp.int32)

    def dp_shift(x, s):
        return lax.ppermute(x, "dp", [(i, (i + s) % n_dp) for i in range(n_dp)])

    def layer_shift(x, k):
        step = SIDE * CORE * k
        return lax.ppermute(x, "expert", [(i, (i + step) % n_experts) for i in range(n_experts)])

    def joint(x, s, moved):
        pairs = [
            (d * n_experts + e, (d + s) % n_dp * n_experts + moved(e)) for d in range(n_dp) for e in range(n_experts)
        ]
        return lax.ppermute(x, ("dp", "expert"), pairs)

    def swap(x, bit):
        return lax.ppermute(x, "expert", [(i, i ^ bit) for i in range(n_experts)])

    index_rows = expert_index.T
    blocks = call(
        functools.partial(pack_kernel, n_dp, n_experts, half),
        [((tok, wide), BF16)] * n_dp,
        (ids, route_weight.T, index_rows),
        far=(tokens, upstream),
        copies=2 * n_dp,
        params=WIDE,
    )
    mine = jnp.concatenate([blocks[0]] + [dp_shift(blocks[s], s) for s in range(1, n_dp)], axis=0)
    wg, wu, wd = call(load_kernel, [((half, ff), BF16)] * 3, (ids,), far=(wg, wu, wd), copies=3)

    near, sides, parts, kept, crossed = [mine], [], [], [], []
    hidden_rows, partials, homes = [], [], []
    order = [k for k in (0, 2, 1, 3) if k < layers] + list(range(4, layers))

    def over_dp(part):
        if len(crossed) >= WINDOW:
            part = after(part, crossed[-WINDOW])
        others = [dp_shift(part, s) for s in range(1, n_dp)]
        crossed.extend(others[-1:])
        return [part] + others

    def forward(i):
        if i == 0:
            sides.append(jnp.concatenate([joint(blocks[s], s, lambda e: e ^ CORE) for s in range(n_dp)], axis=0))
        else:
            sides.append(swap(near[i], CORE))
        both = jnp.concatenate([near[i], sides[i]], axis=0)
        if i + 1 < layers:
            if i == 0:
                step = SIDE * CORE * order[1]
                direct = [joint(blocks[s], s, lambda e: (e + step) % n_experts) for s in range(n_dp)]
                near.append(jnp.concatenate(direct, axis=0))
            else:
                near.append(layer_shift(after(mine, near[i]), order[i + 1]))
        if i == 0:
            both = after(both, wg, wu, wd)
        core = swap(both, 1)
        *pieces, up_rows, sel, weight = call(
            functools.partial(forward_kernel, n_dp, n_experts, tok, cap),
            [
                *[((rows // PIECE_ROWS, 3 * ff // PIECE_COLS), BF16)] * PIECES,
                ((rows, half), BF16),
                ((rows, total), BF16),
                ((rows, LANES), F32),
            ],
            (ids, near[i], sides[i], core, wg, wu, wd),
            flops=2 * rows * half * 3 * ff + 4 * rows * total * half,
        )
        kept.append((up_rows, sel, weight))
        parts.append(sum([over_dp(piece) for piece in pieces], []))

    def backward(i):
        up_rows, sel, weight = kept[i]
        if i + 1 < len(kept):
            weight = after(weight, kept[i + 1][2])
        keep, send, hidden = call(
            functools.partial(backward_kernel, n_experts, n_dp),
            [((total // 2, wide), BF16), ((total // 2, wide), BF16), ((rows, ff), BF16)],
            (ids, *parts[i], sel, weight, wg, wu, wd),
            flops=2 * total * half * 3 * ff + 2 * rows * total * 3 * ff,
        )
        hidden_rows.append(hidden)
        back = swap(send, 1)
        outward = swap(added(keep[group:], back[group:]), CORE)
        partials.append(added(added(keep[:group], back[:group]), outward))
        homes.append(layer_shift(partials[i], -order[i]) if order[i] else partials[i])

    for i in range(layers + 2):
        if i >= 2:
            backward(i - 2)
        if i < layers:
            forward(i)

    (down_grad,) = call(
        functools.partial(down_kernel, layers),
        [((half, ff), BF16)],
        (ids, *[rows_of[0] for rows_of in kept], *hidden_rows),
        flops=2 * layers * rows * half * ff,
    )
    result = sum(partial.astype(F32) for partial in homes)
    result = result.astype(BF16)
    others = [dp_shift(result[s * tok : (s + 1) * tok, : 2 * half], -s) for s in range(1, n_dp)]
    combined, token_grad, route_grad = call(
        functools.partial(final_kernel, n_dp, n_experts, half),
        [((tok, width), BF16), ((tok, width), BF16), ((top, tok), F32)],
        (ids, result[:tok], index_rows, *others),
    )
    return (combined, token_grad, route_grad.T, down_grad[None])


def solution(mesh):
    return jax.shard_map(
        on_device,
        mesh=mesh,
        in_specs=(
            P(("dp", "expert"), None),
            P(("dp", "expert"), None),
            P(("dp", "expert"), None),
            P(("dp", "expert"), None),
            P("expert", "dp", None),
            P("expert", "dp", None),
            P("expert", "dp", None),
        ),
        out_specs=(
            P(("dp", "expert"), None),
            P(("dp", "expert"), None),
            P(("dp", "expert"), None),
            P("expert", "dp", None),
        ),
        check_vma=False,
    )
```
